32 devices in a mesh: seq: 8 (over y, x, core), fsdp: 4 (over z).
Axes of the slice: x: 2, y: 2, z: 4, core: 2. Of those that a mesh axis runs over, the one named last changes fastest.
Arguments:
- tokens: bfloat16 [4, 1024, 768], P('fsdp', 'seq'), may hold values from -6 to 6
- pair_held: int32 [8], replicated, may hold values from 0 to 7, each once
- joint_weight: bfloat16 [768, 2304], P(None, ('seq', 'fsdp')), may hold values from -0.21875 to 0.21875
- joint_bias: bfloat16 [2304], P(('seq', 'fsdp')), may hold values from -3 to 3
- dense_weight: bfloat16 [768, 768], P(('seq', 'fsdp')), may hold values from -3.5 to 3.5
- dense_bias: bfloat16 [768], P(('seq', 'fsdp')), may hold values from -2 to 2
- expand_weight: bfloat16 [768, 3072], P(None, ('seq', 'fsdp')), may hold values from -0.21875 to 0.21875
- expand_bias: bfloat16 [3072], P(('seq', 'fsdp')), may hold values from -3 to 3
- reduce_weight: bfloat16 [3072, 768], P(('seq', 'fsdp')), may hold values from -0.109375 to 0.109375
- reduce_bias: bfloat16 [768], P(('seq', 'fsdp')), may hold values from -2 to 2
- first_gain: bfloat16 [768], P(('seq', 'fsdp')), may hold values from 0.5 to 1.5
- first_shift: bfloat16 [768], P(('seq', 'fsdp')), may hold values from -1 to 1
- second_gain: bfloat16 [768], P(('seq', 'fsdp')), may hold values from 0.5 to 1.5
- second_shift: bfloat16 [768], P(('seq', 'fsdp')), may hold values from -1 to 1
- cotangent: bfloat16 [4, 1024, 768], P('fsdp', 'seq'), may hold values from -6 to 6
Outputs:
- layer_output: bfloat16 [4, 1024, 768], P('fsdp', 'seq')
- input_grad: bfloat16 [4, 1024, 768], P('fsdp', 'seq')
- grad_joint_weight: float32 [768, 2304], P(None, ('seq', 'fsdp'))
- grad_joint_bias: float32 [2304], P(('seq', 'fsdp'))
- grad_dense_weight: float32 [768, 768], P(('seq', 'fsdp'))
- grad_dense_bias: float32 [768], P(('seq', 'fsdp'))
- grad_expand_weight: float32 [768, 3072], P(None, ('seq', 'fsdp'))
- grad_expand_bias: float32 [3072], P(('seq', 'fsdp'))
- grad_reduce_weight: float32 [3072, 768], P(('seq', 'fsdp'))
- grad_reduce_bias: float32 [768], P(('seq', 'fsdp'))
- grad_first_gain: float32 [768], P(('seq', 'fsdp'))
- grad_first_shift: float32 [768], P(('seq', 'fsdp'))
- grad_second_gain: float32 [768], P(('seq', 'fsdp'))
- grad_second_shift: float32 [768], P(('seq', 'fsdp'))
The draws below stay inside these ranges and needn't reach their ends.
Inputs may be any that keep to these rules, and one draw needn't show every extreme that they name: Index d of seq holds blocks pair_held[d] and 15 - pair_held[d] of every sequence, in that order; every pair is held once.
All inputs are finite; a program needn't handle non-finite values.
Results may differ from the reference program's by a relative error of at most 0.012.
Values may be sent and summed in bfloat16 or wider, within the bound.
A program may use at most 128 MiB of HBM per device.

```python
import jax
import jax.numpy as jnp
from jax import lax

D = 768
H = 12
HD = 64
ROT = 16
FF = 3072
BLK = 64
SEQ_LEN = 1024
SEQS = 4
N_SEQ = 8


def block_levels(rng, shape, cuts, least, high):
    def one(dim, blocks):
        steps = jax.random.uniform(jax.random.fold_in(jax.random.fold_in(rng, 6), dim), (blocks,), jnp.float32, least / len(cuts), high / len(cuts))
        return jnp.repeat(jnp.exp(steps), shape[dim] // blocks).reshape((-1,) + (1,) * (len(shape) - dim - 1))

    loudness = one(*cuts[0])
    for cut in cuts[1:]:
        loudness = loudness * one(*cut)
    return loudness


def scatter_about(own_key, shape, scale, limit, pieces=(), kind=jnp.bfloat16):
    values = jax.random.normal(own_key, shape, jnp.float32) * scale
    if len(pieces) > 0:
        values = block_levels(own_key, shape, pieces, -0.22, 0.18) * values
    return jnp.clip(values, min=-limit, max=limit).astype(kind)


def setup_inputs(seed: int = 0) -> dict:
    key_list = jax.random.split(jax.random.key(seed), 16)
    return {
        "tokens": scatter_about(key_list[0], (SEQS, SEQ_LEN, D), 1.0, 6.0, ((0, 4), (1, 8))),
        "pair_held": jax.random.permutation(key_list[1], N_SEQ).astype(jnp.int32),
        "joint_weight": scatter_about(key_list[2], (D, 3 * D), D ** -0.5, 0.21875, ((1, 32),)),
        "joint_bias": scatter_about(key_list[3], (3 * D,), 0.5, 3.0, ((0, 32),)),
        "dense_weight": scatter_about(key_list[4], (D, D), (max(1, 4 * D // SEQ_LEN)) ** -0.5, 3.5, ((0, 32),)),
        "dense_bias": scatter_about(key_list[5], (D,), 0.3, 2.0, ((0, 32),)),
        "expand_weight": scatter_about(key_list[6], (D, FF), D ** -0.5, 0.21875, ((1, 32),)),
        "expand_bias": scatter_about(key_list[7], (FF,), 0.5, 3.0, ((0, 32),)),
        "reduce_weight": scatter_about(key_list[8], (FF, D), FF ** -0.5, 0.109375, ((0, 32),)),
        "reduce_bias": scatter_about(key_list[9], (D,), 0.3, 2.0, ((0, 32),)),
        "first_gain": jnp.clip(1.0 + 0.1 * jax.random.normal(key_list[10], (D,), jnp.float32), 0.5, 1.5).astype(jnp.bfloat16),
        "first_shift": scatter_about(key_list[11], (D,), 0.2, 1.0, ((0, 32),)),
        "second_gain": jnp.clip(1.0 + 0.1 * jax.random.normal(key_list[12], (D,), jnp.float32), 0.5, 1.5).astype(jnp.bfloat16),
        "second_shift": scatter_about(key_list[13], (D,), 0.2, 1.0, ((0, 32),)),
        "cotangent": scatter_about(key_list[14], (SEQS, SEQ_LEN, D), 1.0, 6.0, ((0, 4), (1, 8))),
    }


norm_eps = 1e-05
highest = lax.Precision.HIGHEST

@jax.custom_vjp
def low(v):
    return lax.optimization_barrier(v.astype(jnp.bfloat16)).astype(jnp.float32)

@jax.custom_vjp
def low_back(v):
    return v

def low_keep(v):
    return (low(v), None)

def low_pass(kept, grad):
    return (grad,)

def back_keep(v):
    return (v, None)

def back_low(kept, grad):
    return (low(grad),)
low.defvjp(low_keep, low_pass)
low_back.defvjp(back_keep, back_low)

def layer_norm(values, gain_vec, shift_vec):
    center = values - lax.optimization_barrier(jnp.mean(values, axis=-1, keepdims=True))
    spread = lax.optimization_barrier(jnp.mean(center * center, axis=-1, keepdims=True))
    return center * lax.rsqrt(spread + norm_eps) * gain_vec + shift_vec

def places_of(pair_held, length, block_rows):
    pair_count = pair_held.shape[0]
    row_index = jnp.arange(length, dtype=jnp.int32)
    chosen = pair_held[row_index // (2 * block_rows)]
    block_index = jnp.where(row_index // block_rows % 2 == 0, chosen, 2 * pair_count - 1 - chosen)
    return (block_index * block_rows + row_index % block_rows).astype(jnp.int32)

def rotate(values, places):
    half_rot = ROT // 2
    inverse_freq = 1.0 / 10000.0 ** (jnp.arange(0, ROT, 2, dtype=jnp.float32) / ROT)
    angles = places.astype(jnp.float32)[:, None] * inverse_freq[None, :]
    cosine = jnp.cos(angles)[:, None, :]
    sine_term = jnp.sin(angles)[:, None, :]
    lower_half = values[..., :half_rot]
    upper_half = values[..., half_rot:ROT]
    return jnp.concatenate([lower_half * cosine - upper_half * sine_term, upper_half * cosine + lower_half * sine_term, values[..., ROT:]], axis=-1)

def attend(queries, keys, values, places):
    scores = jnp.einsum('qhd,khd->hqk', queries, keys, precision=highest) * HD ** (-0.5)
    scores = low_back(scores)
    allowed = places[:, None] >= places[None, :]
    scores = jnp.where(allowed[None], scores, -1e+30)
    probs_full = jax.nn.softmax(scores, axis=-1)
    return jnp.einsum('hqk,khd->qhd', low(probs_full), values, precision=highest)

def forward(inputs, joint_weight, joint_bias, dense_weight, dense_bias, expand_weight, expand_bias, reduce_weight, reduce_bias, first_gain, first_shift, second_gain, second_shift, places):
    seq_count, length, features = inputs.shape
    flat_rows = inputs.reshape(seq_count * length, features)
    normed_first = low(layer_norm(flat_rows, first_gain, first_shift))
    projected = low_back(jnp.dot(normed_first, joint_weight, precision=highest) + joint_bias)
    projected = projected.reshape(seq_count, length, H, 3, HD)
    queries = low(rotate(projected[:, :, :, 0], places))
    keys = low(rotate(projected[:, :, :, 1], places))
    values = low(projected[:, :, :, 2])

    def one_sequence(triple):
        return attend(triple[0], triple[1], triple[2], places)
    context = lax.map(jax.checkpoint(one_sequence), (queries, keys, values))
    context_low = low(low_back(context.reshape(seq_count * length, features)))
    branch_attn = jnp.dot(context_low, dense_weight, precision=highest) + dense_bias
    normed_second = low(layer_norm(flat_rows, second_gain, second_shift))
    hidden = low_back(jnp.dot(normed_second, expand_weight, precision=highest) + expand_bias)
    active = low(jax.nn.gelu(hidden, approximate=False))
    branch_mlp = jnp.dot(active, reduce_weight, precision=highest) + reduce_bias
    return (flat_rows + branch_attn + branch_mlp).reshape(seq_count, length, features)

def reference(tokens, pair_held, joint_weight, joint_bias, dense_weight, dense_bias, expand_weight, expand_bias, reduce_weight, reduce_bias, first_gain, first_shift, second_gain, second_shift, cotangent):
    places = places_of(pair_held, tokens.shape[1], BLK)

    def apply(inputs, w_joint, b_joint, w_dense, b_dense, w_expand, b_expand, w_reduce, b_reduce, g_first, s_first, g_second, s_second):
        return forward(inputs, w_joint, b_joint, w_dense, b_dense, w_expand, b_expand, w_reduce, b_reduce, g_first, s_first, g_second, s_second, places)
    result, pullback = jax.vjp(apply, tokens.astype(jnp.float32), joint_weight.astype(jnp.float32), joint_bias.astype(jnp.float32), dense_weight.astype(jnp.float32), dense_bias.astype(jnp.float32), expand_weight.astype(jnp.float32), expand_bias.astype(jnp.float32), reduce_weight.astype(jnp.float32), reduce_bias.astype(jnp.float32), first_gain.astype(jnp.float32), first_shift.astype(jnp.float32), second_gain.astype(jnp.float32), second_shift.astype(jnp.float32))
    grads = pullback(cotangent.astype(jnp.float32))
    return (result.astype(jnp.bfloat16), grads[0].astype(jnp.bfloat16), grads[1], grads[2], grads[3], grads[4], grads[5], grads[6], grads[7], grads[8], grads[9], grads[10], grads[11], grads[12])
```

```python
import math

import jax
import jax.numpy as jnp
from jax import lax
from jax.experimental import pallas as pl
from jax.experimental.pallas import tpu as pltpu
from jax.sharding import PartitionSpec as P

HD = 64
ROT = 16
EPS = 1e-05
MASKED = -1e30
MESH = pl.DeviceIdType.MESH
BF = jnp.bfloat16
F32 = jnp.float32


def greet(peers):
    barrier = pltpu.get_barrier_semaphore()
    for peer in peers:
        pl.semaphore_signal(barrier, inc=1, device_id=peer, device_id_type=MESH)
    pl.semaphore_wait(barrier, len(peers))


def gather_kernel(N, F, G, xg, wa, wb, vec, xg_all, wa_all, wb_all, vec_all, send, recv, local):
    s, f = lax.axis_index("seq"), lax.axis_index("fsdp")
    grp, g = s // G, s % G
    seq_peers = [(lax.rem(s + k, N), f) for k in range(1, N)]
    z_peers = [(s, lax.rem(f + k, F)) for k in range(1, F)]
    mates = [(grp * G + lax.rem(g + k, G), f) for k in range(1, G)]
    greet(seq_peers + z_peers)
    count = [0]

    def push(src, dst, peer):
        i = count[0]
        count[0] += 1
        copy = pltpu.make_async_remote_copy(
            src_ref=src, dst_ref=dst, send_sem=send.at[i], recv_sem=recv.at[i],
            device_id=peer, device_id_type=MESH,
        )
        copy.start()
        return copy

    own = [
        pltpu.make_async_copy(xg, xg_all.at[s], local.at[0]),
        pltpu.make_async_copy(wa, wa_all.at[g, f], local.at[1]),
        pltpu.make_async_copy(wb, wb_all.at[f], local.at[2]),
        pltpu.make_async_copy(vec, vec_all.at[s, f], local.at[3]),
    ]
    for copy in own:
        copy.start()
    vecs = [push(vec, vec_all.at[s, f], peer) for peer in z_peers]
    firsts = [push(wa, wa_all.at[g, f], peer) for peer in z_peers]
    rest = [push(xg, xg_all.at[s], peer) for peer in seq_peers]
    rest += [push(wb, wb_all.at[f], peer) for peer in z_peers]
    for copy in own:
        copy.wait()
    for copy in vecs:
        copy.wait()
    rest += [push(vec_all.at[s], vec_all.at[s], peer) for peer in seq_peers]
    for copy in firsts:
        copy.wait()
    rest += [push(wa_all.at[g], wa_all.at[g], peer) for peer in mates]
    for copy in rest:
        copy.wait()


def scatter_kernel(
    N, F, G, outp, tp, ga, gb, vecp, outr, tr, gar, gbr, vecr, ga_in, ga_sum, vec_in, vec_sum, send, recv
):
    s, f = lax.axis_index("seq"), lax.axis_index("fsdp")
    grp, g = s // G, s % G
    seq_index = [lax.rem(s + k, N) for k in range(1, N)]
    z_index = [lax.rem(f + k, F) for k in range(1, F)]
    mate_index = [lax.rem(g + k, G) for k in range(1, G)]
    greet([(p, f) for p in seq_index] + [(s, p) for p in z_index])
    count = [0]

    def push(src, dst, peer):
        i = count[0]
        count[0] += 1
        copy = pltpu.make_async_remote_copy(
            src_ref=src, dst_ref=dst, send_sem=send.at[i], recv_sem=recv.at[i],
            device_id=peer, device_id_type=MESH,
        )
        copy.start()
        return copy

    vecs = [push(vecp.at[p], vec_in.at[k], (p, f)) for k, p in enumerate(seq_index)]
    mates = [push(ga.at[p], ga_in.at[k], (grp * G + p, f)) for k, p in enumerate(mate_index)]
    rest = [push(gb.at[p], gbr.at[f], (s, p)) for p in z_index]
    for p in seq_index:
        rest.append(push(outp.at[p], outr.at[s], (p, f)))
        rest.append(push(tp.at[p], tr.at[s], (p, f)))
    outr[s] = outp[s]
    tr[s] = tp[s]
    gbr[f] = gb[f]
    for copy in vecs:
        copy.wait()
    total = vecp[s]
    for k in range(N - 1):
        total = total + vec_in[k]
    vec_sum[...] = total
    rest += [push(vec_sum.at[p], vecr.at[f], (s, p)) for p in z_index]
    vecr[f] = vec_sum[f]
    for copy in mates:
        copy.wait()
    for i in range(F):
        part = ga[g, i].astype(F32)
        for k in range(G - 1):
            part = part + ga_in[k, i].astype(F32)
        ga_sum[i] = part.astype(BF)
    rest += [push(ga_sum.at[p], gar.at[f], (s, p)) for p in z_index]
    gar[f] = ga_sum[f]
    for copy in rest:
        copy.wait()


def gather_phase(N, F, G, xg, wa, wb, vec):
    copies = 3 * (F - 1) + 2 * (N - 1) + G - 1
    hbm = pl.BlockSpec(memory_space=pl.ANY)
    return pl.pallas_call(
        lambda *refs: gather_kernel(N, F, G, *refs),
        out_shape=(
            jax.ShapeDtypeStruct((N,) + xg.shape, xg.dtype),
            jax.ShapeDtypeStruct((G, F) + wa.shape, wa.dtype),
            jax.ShapeDtypeStruct((F,) + wb.shape, wb.dtype),
            jax.ShapeDtypeStruct((N, F) + vec.shape, vec.dtype),
        ),
        in_specs=[hbm] * 4,
        out_specs=(hbm,) * 4,
        scratch_shapes=[
            pltpu.SemaphoreType.DMA((copies,)),
            pltpu.SemaphoreType.DMA((copies,)),
            pltpu.SemaphoreType.DMA((4,)),
        ],
        compiler_params=pltpu.CompilerParams(collective_id=0, has_side_effects=True),
    )(xg, wa, wb, vec)


def scatter_phase(N, F, G, outp, tp, ga, gb, vecp):
    copies = 3 * (F - 1) + 3 * (N - 1) + G - 1
    vmem = pl.BlockSpec(memory_space=pltpu.VMEM)
    return pl.pallas_call(
        lambda *refs: scatter_kernel(N, F, G, *refs),
        out_shape=(
            jax.ShapeDtypeStruct(outp.shape, BF),
            jax.ShapeDtypeStruct(tp.shape, BF),
            jax.ShapeDtypeStruct(ga.shape[1:], BF),
            jax.ShapeDtypeStruct(gb.shape, BF),
            jax.ShapeDtypeStruct(vecp.shape[1:], F32),
        ),
        in_specs=[vmem] * 5,
        out_specs=(vmem,) * 5,
        scratch_shapes=[
            pltpu.VMEM((max(G - 1, 1),) + ga.shape[1:], BF),
            pltpu.VMEM(ga.shape[1:], BF),
            pltpu.VMEM((N - 1,) + vecp.shape[1:], F32),
            pltpu.VMEM(vecp.shape[1:], F32),
            pltpu.SemaphoreType.DMA((copies,)),
            pltpu.SemaphoreType.DMA((copies,)),
        ],
        compiler_params=pltpu.CompilerParams(
            collective_id=1, has_side_effects=True, vmem_limit_bytes=48 * 2**20
        ),
    )(outp, tp, ga, gb, vecp)


def row_places(pair_held, count, block_rows):
    pair_count = pair_held.shape[0]
    blocks = jnp.stack([pair_held, 2 * pair_count - 1 - pair_held], axis=1).reshape(-1)
    inside = jnp.arange(block_rows, dtype=jnp.int32)
    return (blocks[:, None] * block_rows + inside[None, :]).reshape(count)


def turn(values, cosine, sine):
    half = ROT // 2
    low, high = values[..., :half], values[..., half:ROT]
    return jnp.concatenate(
        [low * cosine - high * sine, high * cosine + low * sine, values[..., ROT:]], axis=-1
    )


def nt(left, right):
    return lax.dot_general(left, right, (((1,), (1,)), ((), ())), preferred_element_type=F32)


def nn(left, right):
    return jnp.dot(left, right, preferred_element_type=F32)


def tn(left, right):
    return lax.dot_general(left, right, (((0,), (0,)), ((), ())), preferred_element_type=F32)


def pad_rows(array, axis, multiple=16):
    extra = -array.shape[axis] % multiple
    if extra == 0:
        return array
    widths = [(0, 0)] * array.ndim
    widths[axis] = (0, extra)
    return jnp.pad(array, widths)


def make_body(N, F):
    def body(
        tokens, pair_held, joint_weight, joint_bias, dense_weight, dense_bias, expand_weight,
        expand_bias, reduce_weight, reduce_bias, first_gain, first_shift, second_gain,
        second_shift, cotangent,
    ):
        _, R, D = tokens.shape
        L = N * R
        H = D // HD
        G = N // math.gcd(N, H)
        HG = H * G // N
        W = HG * HD
        Q = L // G
        cj, cd, ce = joint_weight.shape[1], dense_weight.shape[0], expand_weight.shape[1]
        s = lax.axis_index("seq")
        grp, gi = s // G, s % G
        scale = HD ** (-0.5)

        xg = jnp.concatenate([tokens, cotangent], axis=0)
        wa = pad_rows(jnp.concatenate([joint_weight.T, dense_weight], axis=0), 0)
        wb = pad_rows(jnp.concatenate([expand_weight.T, reduce_weight], axis=0), 0)
        vec = jnp.concatenate(
            [first_gain, first_shift, second_gain, second_shift, joint_bias, dense_bias,
             expand_bias, reduce_bias]
        ).astype(F32)
        vec = jnp.pad(vec, (0, 1024 - vec.shape[0])).reshape(8, 128)
        xg_all, wa_all, wb_all, vec_all = gather_phase(N, F, G, xg, wa, wb, vec)

        va = vec_all.reshape(N * F, 1024)
        gain1, shift1, gain2, shift2 = [
            va[:, i * cd:(i + 1) * cd].reshape(D) for i in range(4)
        ]
        at = 4 * cd
        bias_j = lax.dynamic_slice_in_dim(va[:, at:at + cj], grp * G * F, G * F, 0).reshape(HG, 3, HD)
        at += cj
        bias_d = va[:, at:at + cd].reshape(D)
        at += cd
        bias_e = lax.dynamic_slice_in_dim(va[:, at:at + ce], s * F, F, 0).reshape(F * ce)
        at += ce
        bias_r = va[:, at:at + cd].reshape(D)

        joint = wa_all[:, :, :cj].reshape(HG, 3, HD, D)
        wq, wk, wv = [joint[:, i].reshape(W, D) for i in range(3)]
        dense = wa_all[:, :, cj:cj + cd].reshape(W, D)
        expand = wb_all[:, :ce].reshape(F * ce, D)
        reduce_w = wb_all[:, ce:2 * ce].reshape(F * ce, D)

        x = xg_all[:, 0].reshape(L, D).astype(F32)
        grad = xg_all[:, 1].reshape(L, D)
        center = x - jnp.mean(x, axis=-1, keepdims=True)
        inv = lax.rsqrt(jnp.mean(center * center, axis=-1, keepdims=True) + EPS)
        n = center * inv
        nf1 = (n * gain1 + shift1).astype(BF)
        nf2 = (n * gain2 + shift2).astype(BF)

        def mine(array):
            return lax.dynamic_slice_in_dim(array, gi * Q, Q, 0)

        def own_rows(array):
            pick = (jnp.arange(G) == gi)[:, None, None]
            return jnp.where(pick, array[None], 0.0).reshape(L, D)

        places = row_places(pair_held, L, R // 2)
        freq = 1.0 / 10000.0 ** (jnp.arange(0, ROT, 2, dtype=F32) / ROT)
        angles = places.astype(F32)[:, None] * freq[None, :]
        cosine, sine = jnp.cos(angles)[:, None], jnp.sin(angles)[:, None]
        cos_q, sin_q, places_q = mine(cosine), mine(sine), mine(places)

        nf1_q, grad_q = mine(nf1), mine(grad)
        q = turn(nt(nf1_q, wq).reshape(Q, HG, HD) + bias_j[:, 0], cos_q, sin_q).astype(BF)
        k = turn(nt(nf1, wk).reshape(L, HG, HD) + bias_j[:, 1], cosine, sine).astype(BF)
        v = (nt(nf1, wv).reshape(L, HG, HD) + bias_j[:, 2]).astype(BF)
        gctx = nt(grad_q, dense).astype(BF).reshape(Q, HG, HD)

        allowed = places_q[:, None] >= places[None, :]
        scores = jnp.einsum("qhd,khd->hqk", q, k, preferred_element_type=F32) * scale
        scores = jnp.where(allowed, scores, MASKED)
        peak = jnp.max(scores, axis=-1, keepdims=True)
        weight = jnp.exp(scores - peak)
        probs_full = weight / jnp.sum(weight, axis=-1, keepdims=True)
        probs = probs_full.astype(BF)
        context = jnp.einsum("hqk,khd->qhd", probs, v, preferred_element_type=F32)
        ctx_low = context.reshape(Q, W).astype(BF)
        g_probs = jnp.einsum("qhd,khd->hqk", gctx, v, preferred_element_type=F32)
        delta = jnp.sum(probs_full * g_probs, axis=-1, keepdims=True)
        g_scores = (probs_full * (g_probs - delta)).astype(BF)
        gq = jnp.einsum("hqk,khd->qhd", g_scores, k, preferred_element_type=F32) * scale
        gk = jnp.einsum("hqk,qhd->khd", g_scores, q, preferred_element_type=F32) * scale
        gv = jnp.einsum("hqk,qhd->khd", probs, gctx, preferred_element_type=F32)
        gq = turn(gq, cos_q, -sin_q).astype(BF).reshape(Q, W)
        gk = turn(gk, cosine, -sine).astype(BF).reshape(L, W)
        gv = gv.astype(BF).reshape(L, W)

        hidden = nt(nf2, expand) + bias_e
        active, gelu_pull = jax.vjp(lambda t: jax.nn.gelu(t, approximate=False), hidden)
        active = active.astype(BF)
        out_part = nn(active, reduce_w) + own_rows(nn(ctx_low, dense))
        g_hidden = gelu_pull(nt(grad, reduce_w))[0].astype(BF)
        g2 = nn(g_hidden, expand)
        g1 = nn(gk, wk) + nn(gv, wv) + own_rows(nn(gq, wq))
        t_part = g1 * gain1 + g2 * gain2

        d_joint = jnp.stack(
            [tn(gq, nf1_q).astype(BF).reshape(HG, HD, D), tn(gk, nf1).astype(BF).reshape(HG, HD, D),
             tn(gv, nf1).astype(BF).reshape(HG, HD, D)], axis=1
        ).reshape(G, F, cj, D)
        d_dense = tn(ctx_low, grad_q).astype(BF).reshape(G, F, cd, D)
        ga = pad_rows(jnp.concatenate([d_joint, d_dense], axis=2), 2)
        gb = pad_rows(
            jnp.concatenate(
                [tn(g_hidden, nf2).astype(BF).reshape(F, ce, D),
                 tn(active, grad).astype(BF).reshape(F, ce, D)], axis=1), 1
        )

        def col(array):
            return jnp.sum(array.astype(F32), axis=0)

        owner_s = jnp.arange(N * F) // F
        gains = [
            p.reshape(N * F, cd)
            for p in (jnp.sum(g1 * n, axis=0), jnp.sum(g1, axis=0), jnp.sum(g2 * n, axis=0), jnp.sum(g2, axis=0))
        ]
        b_joint = jnp.stack([col(a).reshape(HG, HD) for a in (gq, gk, gv)], axis=1).reshape(G * F, cj)
        b_joint = lax.dynamic_update_slice_in_dim(jnp.zeros((N * F, cj), F32), b_joint, grp * G * F, 0)
        b_expand = lax.dynamic_update_slice_in_dim(
            jnp.zeros((N * F, ce), F32), col(g_hidden).reshape(F, ce), s * F, 0
        )
        b_out = jnp.where((owner_s == s)[:, None], col(grad).reshape(N * F, cd), 0.0)
        vecp = jnp.concatenate(gains + [b_joint, b_out, b_expand], axis=1)
        vecp = jnp.pad(vecp, ((0, 0), (0, 1024 - vecp.shape[1]))).reshape(N, F, 8, 128)

        outr, tr, gar, gbr, vecr = scatter_phase(
            N, F, G, out_part.astype(BF).reshape(N, R, D), t_part.astype(BF).reshape(N, R, D),
            ga, gb, vecp
        )
        x_own = tokens[0].astype(F32)
        layer_output = (x_own + jnp.sum(outr.astype(F32), axis=0) + bias_d + bias_r).astype(BF)
        center = x_own - jnp.mean(x_own, axis=-1, keepdims=True)
        inv_own = lax.rsqrt(jnp.mean(center * center, axis=-1, keepdims=True) + EPS)
        n_own = center * inv_own
        t = jnp.sum(tr.astype(F32), axis=0)
        g_in = (
            t - jnp.mean(t, axis=-1, keepdims=True)
            - n_own * jnp.mean(t * n_own, axis=-1, keepdims=True)
        ) * inv_own
        input_grad = (cotangent[0].astype(F32) + g_in).astype(BF)
        a = jnp.sum(gar.astype(F32), axis=0)
        b = jnp.sum(gbr.astype(F32), axis=0)
        vs = jnp.sum(vecr, axis=0).reshape(1024)
        at = 4 * cd
        o_joint, at = vs[at:at + cj], at + cj
        o_out, at = vs[at:at + cd], at + cd
        o_expand = vs[at:at + ce]
        return (
            layer_output[None], input_grad[None], a[:cj].T, o_joint, a[cj:cj + cd], o_out,
            b[:ce].T, o_expand, b[ce:2 * ce], o_out,
            vs[:cd], vs[cd:2 * cd], vs[2 * cd:3 * cd], vs[3 * cd:4 * cd],
        )

    return body


def solution(mesh):
    both = ("seq", "fsdp")
    cols, rows, vector = P(None, both), P(both, None), P(both)
    acts = P("fsdp", "seq", None)
    return jax.shard_map(
        make_body(mesh.shape["seq"], mesh.shape["fsdp"]),
        mesh=mesh,
        in_specs=(
            acts, P(), cols, vector, rows, vector, cols, vector, rows, vector,
            vector, vector, vector, vector, acts,
        ),
        out_specs=(
            acts, acts, cols, vector, rows, vector, cols, vector, rows, vector,
            vector, vector, vector, vector,
        ),
        check_vma=False,
    )
```

```python
import math

import jax
import jax.numpy as jnp
from jax import lax
from jax.experimental import pallas as pl
from jax.experimental.pallas import tpu as pltpu
from jax.sharding import PartitionSpec as P

HD = 64
ROT = 16
EPS = 1e-05
MASKED = -1e30
MESH = pl.DeviceIdType.MESH
BF = jnp.bfloat16
F32 = jnp.float32


def greet(peers):
    barrier = pltpu.get_barrier_semaphore()
    for peer in peers:
        pl.semaphore_signal(barrier, inc=1, device_id=peer, device_id_type=MESH)
    pl.semaphore_wait(barrier, len(peers))


def pusher(send, recv):
    count = [0]

    def push(src, dst, peer):
        i = count[0]
        count[0] += 1
        copy = pltpu.make_async_remote_copy(
            src_ref=src, dst_ref=dst, send_sem=send.at[i], recv_sem=recv.at[i],
            device_id=peer, device_id_type=MESH,
        )
        copy.start()
        return copy

    return push


def gather_kernel(N, F, G, xg, wa, vec, xg_all, wa_all, vec_all, send, recv, local):
    s, f = lax.axis_index("seq"), lax.axis_index("fsdp")
    grp, g = s // G, lax.rem(s, G)
    partner = (s + 1 - 2 * lax.rem(s, 2), f)
    seq_peers = [(lax.rem(s + k, N), f) for k in range(1, N)]
    z_peers = [(s, lax.rem(f + k, F)) for k in range(1, F)]
    mates = [(grp * G + lax.rem(g + k, G), f) for k in range(1, G)]
    greet(seq_peers + z_peers)
    push = pusher(send, recv)
    own = [
        pltpu.make_async_copy(xg, xg_all.at[s], local.at[0]),
        pltpu.make_async_copy(wa, wa_all.at[g, f], local.at[1]),
        pltpu.make_async_copy(vec, vec_all.at[s, f], local.at[2]),
    ]
    for copy in own:
        copy.start()
    vecs = [push(vec, vec_all.at[s, f], peer) for peer in z_peers]
    far = [push(xg, xg_all.at[s], (lax.rem(s + k, N), f)) for k in range(2, N, 2)]
    firsts = [push(wa, wa_all.at[g, f], peer) for peer in z_peers]
    rest = [push(xg, xg_all.at[s], partner)]
    for copy in own:
        copy.wait()
    for copy in vecs:
        copy.wait()
    rest += [push(vec_all.at[s], vec_all.at[s], peer) for peer in seq_peers]
    for copy in firsts:
        copy.wait()
    rest += [push(wa_all.at[g], wa_all.at[g], peer) for peer in mates]
    for k, copy in zip(range(2, N, 2), far):
        copy.wait()
        origin = lax.rem(s + N - k, N)
        rest.append(push(xg_all.at[origin], xg_all.at[origin], partner))
    for copy in rest:
        copy.wait()


def scatter_kernel(
    N, F, G, outp, tp, ga, vecp, outr, tr, gar, vecr,
    pair_in, pair_sum, ga_in, ga_sum, vec_in, vec_sum, send, recv
):
    s, f = lax.axis_index("seq"), lax.axis_index("fsdp")
    grp, g = s // G, lax.rem(s, G)
    chip, core = s // 2, lax.rem(s, 2)
    C = N // 2
    partner = (s + 1 - 2 * core, f)
    seq_index = [lax.rem(s + k, N) for k in range(1, N)]
    z_index = [lax.rem(f + k, F) for k in range(1, F)]
    mate_index = [lax.rem(g + k, G) for k in range(1, G)]
    greet([(p, f) for p in seq_index] + [(s, p) for p in z_index])
    push = pusher(send, recv)
    mates = [push(ga.at[p], ga_in.at[k], (grp * G + p, f)) for k, p in enumerate(mate_index)]
    chips = [lax.rem(chip + k, C) for k in range(1, C)] + [chip]
    halves = []
    for j in chips:
        halves.append(
            [push(a.at[2 * j + 1 - core], pair_in.at[i, j], partner) for i, a in enumerate((outp, tp))]
        )
    vecs = [push(vecp.at[p], vec_in.at[k], (p, f)) for k, p in enumerate(seq_index)]
    rest = []
    for copy in mates:
        copy.wait()
    for i in range(F):
        part = ga[g, i].astype(F32)
        for k in range(G - 1):
            part = part + ga_in[k, i].astype(F32)
        ga_sum[i] = part.astype(BF)
    rest += [push(ga_sum.at[p], gar.at[f], (s, p)) for p in z_index]
    waits = []
    for n, j in enumerate(chips):
        for i, (a, out) in enumerate(((outp, outr), (tp, tr))):
            halves[n][i].wait()
            both = (a[2 * j + core].astype(F32) + pair_in[i, j].astype(F32)).astype(BF)
            if n == C - 1:
                out[chip] = both
            else:
                pair_sum[i, j] = both
                waits.append(push(pair_sum.at[i, j], out.at[chip], (2 * j + core, f)))
    gar[f] = ga_sum[f]
    for copy in vecs:
        copy.wait()
    total = vecp[s]
    for k in range(N - 1):
        total = total + vec_in[k]
    vec_sum[...] = total
    rest += [push(vec_sum.at[p], vecr.at[f], (s, p)) for p in z_index]
    vecr[f] = vec_sum[f]
    for copy in rest + waits:
        copy.wait()


COST = pl.CostEstimate(flops=0, bytes_accessed=80 * 10**6, transcendentals=0)


def gather_phase(N, F, G, xg, wa, vec):
    copies = 2 * (F - 1) + 2 * (N - 1) + G - 1
    hbm = pl.BlockSpec(memory_space=pl.ANY)
    return pl.pallas_call(
        lambda *refs: gather_kernel(N, F, G, *refs),
        out_shape=(
            jax.ShapeDtypeStruct((N,) + xg.shape, xg.dtype),
            jax.ShapeDtypeStruct((G, F) + wa.shape, wa.dtype),
            jax.ShapeDtypeStruct((N, F) + vec.shape, vec.dtype),
        ),
        in_specs=[hbm] * 3,
        out_specs=(hbm,) * 3,
        scratch_shapes=[
            pltpu.SemaphoreType.DMA((copies,)),
            pltpu.SemaphoreType.DMA((copies,)),
            pltpu.SemaphoreType.DMA((3,)),
        ],
        compiler_params=pltpu.CompilerParams(collective_id=0, has_side_effects=True),
        cost_estimate=COST,
    )(xg, wa, vec)


def scatter_phase(N, F, G, outp, tp, ga, vecp):
    copies = 2 * (F - 1) + 3 * N + G
    vmem = pl.BlockSpec(memory_space=pltpu.VMEM)
    half = (N // 2,) + outp.shape[1:]
    return pl.pallas_call(
        lambda *refs: scatter_kernel(N, F, G, *refs),
        out_shape=(
            jax.ShapeDtypeStruct(half, BF),
            jax.ShapeDtypeStruct(half, BF),
            jax.ShapeDtypeStruct(ga.shape[1:], BF),
            jax.ShapeDtypeStruct(vecp.shape[1:], F32),
        ),
        in_specs=[vmem] * 4,
        out_specs=(vmem,) * 4,
        scratch_shapes=[
            pltpu.VMEM((2,) + half, BF),
            pltpu.VMEM((2,) + half, BF),
            pltpu.VMEM((max(G - 1, 1),) + ga.shape[1:], BF),
            pltpu.VMEM(ga.shape[1:], BF),
            pltpu.VMEM((N - 1,) + vecp.shape[1:], F32),
            pltpu.VMEM(vecp.shape[1:], F32),
            pltpu.SemaphoreType.DMA((copies,)),
            pltpu.SemaphoreType.DMA((copies,)),
        ],
        compiler_params=pltpu.CompilerParams(
            collective_id=1, has_side_effects=True, vmem_limit_bytes=48 * 2**20
        ),
        cost_estimate=COST,
    )(outp, tp, ga, vecp)


def lane_rows(arrays):
    spread = [jnp.pad(a, [(0, 0)] * (a.ndim - 1) + [(0, 128 - a.shape[-1])]) for a in arrays]
    spread += [jnp.zeros_like(spread[0])] * (8 - len(spread))
    return jnp.stack(spread, axis=-2)


def row_places(pair_held, count, block_rows):
    pair_count = pair_held.shape[0]
    blocks = jnp.stack([pair_held, 2 * pair_count - 1 - pair_held], axis=1).reshape(-1)
    inside = jnp.arange(block_rows, dtype=jnp.int32)
    return (blocks[:, None] * block_rows + inside[None, :]).reshape(count)


def turn(values, cosine, sine):
    half = ROT // 2
    low, high = values[..., :half], values[..., half:ROT]
    return jnp.concatenate(
        [low * cosine - high * sine, high * cosine + low * sine, values[..., ROT:]], axis=-1
    )


def nt(left, right):
    return lax.dot_general(left, right, (((1,), (1,)), ((), ())), preferred_element_type=F32)


def nn(left, right):
    return jnp.dot(left, right, preferred_element_type=F32)


def tn(left, right):
    return lax.dot_general(left, right, (((0,), (0,)), ((), ())), preferred_element_type=F32)


def pad_rows(array, axis, multiple=16):
    extra = -array.shape[axis] % multiple
    if extra == 0:
        return array
    widths = [(0, 0)] * array.ndim
    widths[axis] = (0, extra)
    return jnp.pad(array, widths)


def make_body(N, F):
    def body(
        tokens, pair_held, joint_weight, joint_bias, dense_weight, dense_bias, expand_weight,
        expand_bias, reduce_weight, reduce_bias, first_gain, first_shift, second_gain,
        second_shift, cotangent,
    ):
        _, R, D = tokens.shape
        L = N * R
        H = D // HD
        G = N // math.gcd(N, H)
        HG = H * G // N
        W = HG * HD
        Q = L // G
        cj, cd, ce = joint_weight.shape[1], dense_weight.shape[0], expand_weight.shape[1]
        s, f = lax.axis_index("seq"), lax.axis_index("fsdp")
        grp, gi = s // G, s % G
        scale = HD ** (-0.5)

        xg = jnp.concatenate([tokens, cotangent], axis=0)
        wa = pad_rows(jnp.concatenate([joint_weight.T, dense_weight], axis=0), 0)
        wb = pad_rows(jnp.concatenate([expand_weight.T, reduce_weight], axis=0), 0)
        vec = lane_rows(
            [array.astype(F32) for array in (
                first_gain, first_shift, second_gain, second_shift, joint_bias, dense_bias,
                expand_bias, reduce_bias)]
        )
        wb_list = [wb] + [
            lax.ppermute(wb, "fsdp", [(i, (i + k) % F) for i in range(F)]) for k in range(1, F)
        ]
        xg_all, wa_all, vec_all = gather_phase(N, F, G, xg, wa, vec)

        va = vec_all.reshape(N * F, 8, 128)
        gain1, shift1, gain2, shift2, _, bias_d, _, bias_r = [
            va[:, i, :cd].reshape(D) for i in range(8)
        ]
        bias_j = lax.dynamic_slice_in_dim(va[:, 4, :cj], grp * G * F, G * F, 0).reshape(HG, 3, HD)
        places_f = jnp.arange(F)
        turned = (places_f[None, :] == (f - places_f[:, None] + F) % F)[:, :, None]
        bias_e = lax.dynamic_slice_in_dim(va[:, 6, :ce], s * F, F, 0)
        bias_e = jnp.sum(jnp.where(turned, bias_e[None], 0.0), axis=1).reshape(F * ce)

        joint = wa_all[:, :, :cj].reshape(HG, 3, HD, D)
        wq, wk, wv = [joint[:, i].reshape(W, D) for i in range(3)]
        dense = wa_all[:, :, cj:cj + cd].reshape(W, D)
        expand = jnp.concatenate([w[:ce] for w in wb_list], axis=0)
        reduce_w = jnp.concatenate([w[ce:2 * ce] for w in wb_list], axis=0)

        x = xg_all[:, 0].reshape(L, D).astype(F32)
        grad = xg_all[:, 1].reshape(L, D)
        center = x - jnp.mean(x, axis=-1, keepdims=True)
        inv = lax.rsqrt(jnp.mean(center * center, axis=-1, keepdims=True) + EPS)
        n = center * inv
        nf1 = (n * gain1 + shift1).astype(BF)
        nf2 = (n * gain2 + shift2).astype(BF)

        def mine(array):
            return lax.dynamic_slice_in_dim(array, gi * Q, Q, 0)

        def own_rows(array):
            pick = (jnp.arange(G) == gi)[:, None, None]
            return jnp.where(pick, array[None], 0.0).reshape(L, D)

        places = row_places(pair_held, L, R // 2)
        freq = 1.0 / 10000.0 ** (jnp.arange(0, ROT, 2, dtype=F32) / ROT)
        angles = places.astype(F32)[:, None] * freq[None, :]
        cosine, sine = jnp.cos(angles)[:, None], jnp.sin(angles)[:, None]
        cos_q, sin_q, places_q = mine(cosine), mine(sine), mine(places)

        nf1_q, grad_q = mine(nf1), mine(grad)
        q = turn(nt(nf1_q, wq).reshape(Q, HG, HD) + bias_j[:, 0], cos_q, sin_q).astype(BF)
        k = turn(nt(nf1, wk).reshape(L, HG, HD) + bias_j[:, 1], cosine, sine).astype(BF)
        v = (nt(nf1, wv).reshape(L, HG, HD) + bias_j[:, 2]).astype(BF)
        gctx = nt(grad_q, dense).astype(BF).reshape(Q, HG, HD)

        allowed = places_q[:, None] >= places[None, :]
        scores = jnp.einsum("qhd,khd->hqk", q, k, preferred_element_type=F32) * scale
        scores = jnp.where(allowed, scores, MASKED)
        peak = jnp.max(scores, axis=-1, keepdims=True)
        weight = jnp.exp(scores - peak)
        probs_full = weight / jnp.sum(weight, axis=-1, keepdims=True)
        probs = probs_full.astype(BF)
        context = jnp.einsum("hqk,khd->qhd", probs, v, preferred_element_type=F32)
        ctx_low = context.reshape(Q, W).astype(BF)
        nf2_late, ctx_low = lax.optimization_barrier((nf2, ctx_low))
        hidden = nt(nf2_late, expand) + bias_e
        active, gelu_pull = jax.vjp(lambda t: jax.nn.gelu(t, approximate=False), hidden)
        active = active.astype(BF)
        g_hidden = gelu_pull(nt(grad, reduce_w))[0].astype(BF)
        gb = pad_rows(
            jnp.concatenate(
                [tn(g_hidden, nf2).astype(BF).reshape(F, ce, D),
                 tn(active, grad).astype(BF).reshape(F, ce, D)], axis=1), 1
        )
        gctx, gb = lax.optimization_barrier((gctx, gb))
        b_parts = [gb[0]] + [
            lax.ppermute(gb[k], "fsdp", [(i, (i - k) % F) for i in range(F)]) for k in range(1, F)
        ]
        g_probs = jnp.einsum("qhd,khd->hqk", gctx, v, preferred_element_type=F32)
        delta = jnp.sum(probs_full * g_probs, axis=-1, keepdims=True)
        g_scores = (probs_full * (g_probs - delta)).astype(BF)
        gq = jnp.einsum("hqk,khd->qhd", g_scores, k, preferred_element_type=F32) * scale
        gk = jnp.einsum("hqk,qhd->khd", g_scores, q, preferred_element_type=F32) * scale
        gv = jnp.einsum("hqk,qhd->khd", probs, gctx, preferred_element_type=F32)
        gq = turn(gq, cos_q, -sin_q).astype(BF).reshape(Q, W)
        gk = turn(gk, cosine, -sine).astype(BF).reshape(L, W)
        gv = gv.astype(BF).reshape(L, W)

        out_part = nn(active, reduce_w) + own_rows(nn(ctx_low, dense))
        g2 = nn(g_hidden, expand)
        g1 = nn(gk, wk) + nn(gv, wv) + own_rows(nn(gq, wq))
        t_part = g1 * gain1 + g2 * gain2

        d_joint = jnp.stack(
            [tn(gq, nf1_q).astype(BF).reshape(HG, HD, D), tn(gk, nf1).astype(BF).reshape(HG, HD, D),
             tn(gv, nf1).astype(BF).reshape(HG, HD, D)], axis=1
        ).reshape(G, F, cj, D)
        d_dense = tn(ctx_low, grad_q).astype(BF).reshape(G, F, cd, D)
        ga = pad_rows(jnp.concatenate([d_joint, d_dense], axis=2), 2)

        def col(array):
            return jnp.sum(array.astype(F32), axis=0)

        owner_s = jnp.arange(N * F) // F
        gains = [
            p.reshape(N * F, cd)
            for p in (jnp.sum(g1 * n, axis=0), jnp.sum(g1, axis=0), jnp.sum(g2 * n, axis=0), jnp.sum(g2, axis=0))
        ]
        b_joint = jnp.stack([col(a).reshape(HG, HD) for a in (gq, gk, gv)], axis=1).reshape(G * F, cj)
        b_joint = lax.dynamic_update_slice_in_dim(jnp.zeros((N * F, cj), F32), b_joint, grp * G * F, 0)
        b_expand = lax.dynamic_update_slice_in_dim(
            jnp.zeros((N * F, ce), F32),
            jnp.sum(jnp.where(turned, col(g_hidden).reshape(1, F, ce), 0.0), axis=1), s * F, 0
        )
        b_out = jnp.where((owner_s == s)[:, None], col(grad).reshape(N * F, cd), 0.0)
        vecp = lane_rows(gains + [b_joint, b_out, b_expand]).reshape(N, F, 8, 128)

        outr, tr, gar, vecr = scatter_phase(
            N, F, G, out_part.astype(BF).reshape(N, R, D), t_part.astype(BF).reshape(N, R, D),
            ga, vecp
        )
        x_own = tokens[0].astype(F32)
        layer_output = (x_own + jnp.sum(outr.astype(F32), axis=0) + bias_d + bias_r).astype(BF)
        center = x_own - jnp.mean(x_own, axis=-1, keepdims=True)
        inv_own = lax.rsqrt(jnp.mean(center * center, axis=-1, keepdims=True) + EPS)
        n_own = center * inv_own
        t = jnp.sum(tr.astype(F32), axis=0)
        g_in = (
            t - jnp.mean(t, axis=-1, keepdims=True)
            - n_own * jnp.mean(t * n_own, axis=-1, keepdims=True)
        ) * inv_own
        input_grad = (cotangent[0].astype(F32) + g_in).astype(BF)
        a = jnp.sum(gar.astype(F32), axis=0)
        b = sum(part.astype(F32) for part in b_parts)
        vs = jnp.sum(vecr, axis=0)
        o_joint, o_out, o_expand = vs[4, :cj], vs[5, :cd], vs[6, :ce]
        return (
            layer_output[None], input_grad[None], a[:cj].T, o_joint, a[cj:cj + cd], o_out,
            b[:ce].T, o_expand, b[ce:2 * ce], o_out,
            vs[0, :cd], vs[1, :cd], vs[2, :cd], vs[3, :cd],
        )

    return body


def solution(mesh):
    both = ("seq", "fsdp")
    cols, rows, vector = P(None, both), P(both, None), P(both)
    acts = P("fsdp", "seq", None)
    return jax.shard_map(
        make_body(mesh.shape["seq"], mesh.shape["fsdp"]),
        mesh=mesh,
        in_specs=(
            acts, P(), cols, vector, rows, vector, cols, vector, rows, vector,
            vector, vector, vector, vector, acts,
        ),
        out_specs=(
            acts, acts, cols, vector, rows, vector, cols, vector, rows, vector,
            vector, vector, vector, vector,
        ),
        check_vma=False,
    )
```

```python
import math

import jax
import jax.numpy as jnp
from jax import lax
from jax.experimental import pallas as pl
from jax.experimental.pallas import tpu as pltpu
from jax.sharding import PartitionSpec as P

HD = 64
ROT = 16
EPS = 1e-05
MASKED = -1e30
MESH = pl.DeviceIdType.MESH
BF = jnp.bfloat16
F32 = jnp.float32


def greet(peers):
    barrier = pltpu.get_barrier_semaphore()
    for peer in peers:
        pl.semaphore_signal(barrier, inc=1, device_id=peer, device_id_type=MESH)
    pl.semaphore_wait(barrier, len(peers))


def pusher(send, recv):
    count = [0]

    def push(src, dst, peer):
        i = count[0]
        count[0] += 1
        copy = pltpu.make_async_remote_copy(
            src_ref=src, dst_ref=dst, send_sem=send.at[i], recv_sem=recv.at[i],
            device_id=peer, device_id_type=MESH,
        )
        copy.start()
        return copy

    return push


def gather_kernel(N, F, G, xg, wa, wb, vec, xg_all, wa_all, wb_all, vec_all, send, recv, local):
    s, f = lax.axis_index("seq"), lax.axis_index("fsdp")
    grp, g = s // G, lax.rem(s, G)
    partner = (s + 1 - 2 * lax.rem(s, 2), f)
    seq_peers = [(lax.rem(s + k, N), f) for k in range(1, N)]
    z_peers = [(s, lax.rem(f + k, F)) for k in range(1, F)]
    mates = [(grp * G + lax.rem(g + k, G), f) for k in range(1, G)]
    greet(seq_peers + z_peers)
    push = pusher(send, recv)
    own = [
        pltpu.make_async_copy(xg, xg_all.at[s], local.at[0]),
        pltpu.make_async_copy(wa, wa_all.at[g, f], local.at[1]),
        pltpu.make_async_copy(vec, vec_all.at[s, f], local.at[2]),
        pltpu.make_async_copy(wb, wb_all.at[f], local.at[3]),
    ]
    for copy in own:
        copy.start()
    vecs = [push(vec, vec_all.at[s, f], peer) for peer in z_peers]
    far = [push(xg, xg_all.at[s], (lax.rem(s + k, N), f)) for k in range(2, N, 2)]
    firsts = [push(wa, wa_all.at[g, f], peer) for peer in z_peers]
    rest = [push(xg, xg_all.at[s], partner)]
    rest += [push(wb, wb_all.at[f], peer) for peer in z_peers]
    for copy in own:
        copy.wait()
    for copy in vecs:
        copy.wait()
    rest += [push(vec_all.at[s], vec_all.at[s], peer) for peer in seq_peers]
    for copy in firsts:
        copy.wait()
    rest += [push(wa_all.at[g], wa_all.at[g], peer) for peer in mates]
    for k, copy in zip(range(2, N, 2), far):
        copy.wait()
        origin = lax.rem(s + N - k, N)
        rest.append(push(xg_all.at[origin], xg_all.at[origin], partner))
    for copy in rest:
        copy.wait()


def scatter_kernel(
    N, F, G, outp, tp, ga, gb, vecp, outr, tr, gar, gbr, vecr,
    pair_in, pair_sum, ga_in, ga_sum, vec_in, vec_sum, send, recv
):
    s, f = lax.axis_index("seq"), lax.axis_index("fsdp")
    grp, g = s // G, lax.rem(s, G)
    chip, core = s // 2, lax.rem(s, 2)
    C = N // 2
    partner = (s + 1 - 2 * core, f)
    seq_index = [lax.rem(s + k, N) for k in range(1, N)]
    z_index = [lax.rem(f + k, F) for k in range(1, F)]
    mate_index = [lax.rem(g + k, G) for k in range(1, G)]
    greet([(p, f) for p in seq_index] + [(s, p) for p in z_index])
    push = pusher(send, recv)
    mates = [push(ga.at[p], ga_in.at[k], (grp * G + p, f)) for k, p in enumerate(mate_index)]
    chips = [lax.rem(chip + k, C) for k in range(1, C)] + [chip]
    halves = []
    for j in chips:
        halves.append(
            [push(a.at[2 * j + 1 - core], pair_in.at[i, j], partner) for i, a in enumerate((outp, tp))]
        )
    rest = [push(gb.at[p], gbr.at[f], (s, p)) for p in z_index]
    vecs = [push(vecp.at[p], vec_in.at[k], (p, f)) for k, p in enumerate(seq_index)]
    for copy in mates:
        copy.wait()
    for i in range(F):
        part = ga[g, i].astype(F32)
        for k in range(G - 1):
            part = part + ga_in[k, i].astype(F32)
        ga_sum[i] = part.astype(BF)
    rest += [push(ga_sum.at[p], gar.at[f], (s, p)) for p in z_index]
    waits = []
    for n, j in enumerate(chips):
        for i, (a, out) in enumerate(((outp, outr), (tp, tr))):
            halves[n][i].wait()
            both = (a[2 * j + core].astype(F32) + pair_in[i, j].astype(F32)).astype(BF)
            if n == C - 1:
                out[chip] = both
            else:
                pair_sum[i, j] = both
                waits.append(push(pair_sum.at[i, j], out.at[chip], (2 * j + core, f)))
    gar[f] = ga_sum[f]
    gbr[f] = gb[f]
    for copy in vecs:
        copy.wait()
    total = vecp[s]
    for k in range(N - 1):
        total = total + vec_in[k]
    vec_sum[...] = total
    rest += [push(vec_sum.at[p], vecr.at[f], (s, p)) for p in z_index]
    vecr[f] = vec_sum[f]
    for copy in rest + waits:
        copy.wait()


def gather_phase(N, F, G, xg, wa, wb, vec):
    copies = 3 * (F - 1) + 2 * (N - 1) + G - 1
    hbm = pl.BlockSpec(memory_space=pl.ANY)
    return pl.pallas_call(
        lambda *refs: gather_kernel(N, F, G, *refs),
        out_shape=(
            jax.ShapeDtypeStruct((N,) + xg.shape, xg.dtype),
            jax.ShapeDtypeStruct((G, F) + wa.shape, wa.dtype),
            jax.ShapeDtypeStruct((F,) + wb.shape, wb.dtype),
            jax.ShapeDtypeStruct((N, F) + vec.shape, vec.dtype),
        ),
        in_specs=[hbm] * 4,
        out_specs=(hbm,) * 4,
        scratch_shapes=[
            pltpu.SemaphoreType.DMA((copies,)),
            pltpu.SemaphoreType.DMA((copies,)),
            pltpu.SemaphoreType.DMA((4,)),
        ],
        compiler_params=pltpu.CompilerParams(collective_id=0, has_side_effects=True),
    )(xg, wa, wb, vec)


def scatter_phase(N, F, G, outp, tp, ga, gb, vecp):
    copies = 3 * (F - 1) + 3 * N + G
    vmem = pl.BlockSpec(memory_space=pltpu.VMEM)
    half = (N // 2,) + outp.shape[1:]
    return pl.pallas_call(
        lambda *refs: scatter_kernel(N, F, G, *refs),
        out_shape=(
            jax.ShapeDtypeStruct(half, BF),
            jax.ShapeDtypeStruct(half, BF),
            jax.ShapeDtypeStruct(ga.shape[1:], BF),
            jax.ShapeDtypeStruct(gb.shape, BF),
            jax.ShapeDtypeStruct(vecp.shape[1:], F32),
        ),
        in_specs=[vmem] * 5,
        out_specs=(vmem,) * 5,
        scratch_shapes=[
            pltpu.VMEM((2,) + half, BF),
            pltpu.VMEM((2,) + half, BF),
            pltpu.VMEM((max(G - 1, 1),) + ga.shape[1:], BF),
            pltpu.VMEM(ga.shape[1:], BF),
            pltpu.VMEM((N - 1,) + vecp.shape[1:], F32),
            pltpu.VMEM(vecp.shape[1:], F32),
            pltpu.SemaphoreType.DMA((copies,)),
            pltpu.SemaphoreType.DMA((copies,)),
        ],
        compiler_params=pltpu.CompilerParams(
            collective_id=1, has_side_effects=True, vmem_limit_bytes=48 * 2**20
        ),
    )(outp, tp, ga, gb, vecp)


def row_places(pair_held, count, block_rows):
    pair_count = pair_held.shape[0]
    blocks = jnp.stack([pair_held, 2 * pair_count - 1 - pair_held], axis=1).reshape(-1)
    inside = jnp.arange(block_rows, dtype=jnp.int32)
    return (blocks[:, None] * block_rows + inside[None, :]).reshape(count)


def turn(values, cosine, sine):
    half = ROT // 2
    low, high = values[..., :half], values[..., half:ROT]
    return jnp.concatenate(
        [low * cosine - high * sine, high * cosine + low * sine, values[..., ROT:]], axis=-1
    )


def nt(left, right):
    return lax.dot_general(left, right, (((1,), (1,)), ((), ())), preferred_element_type=F32)


def nn(left, right):
    return jnp.dot(left, right, preferred_element_type=F32)


def tn(left, right):
    return lax.dot_general(left, right, (((0,), (0,)), ((), ())), preferred_element_type=F32)


def pad_rows(array, axis, multiple=16):
    extra = -array.shape[axis] % multiple
    if extra == 0:
        return array
    widths = [(0, 0)] * array.ndim
    widths[axis] = (0, extra)
    return jnp.pad(array, widths)


def make_body(N, F):
    def body(
        tokens, pair_held, joint_weight, joint_bias, dense_weight, dense_bias, expand_weight,
        expand_bias, reduce_weight, reduce_bias, first_gain, first_shift, second_gain,
        second_shift, cotangent,
    ):
        _, R, D = tokens.shape
        L = N * R
        H = D // HD
        G = N // math.gcd(N, H)
        HG = H * G // N
        W = HG * HD
        Q = L // G
        cj, cd, ce = joint_weight.shape[1], dense_weight.shape[0], expand_weight.shape[1]
        s = lax.axis_index("seq")
        grp, gi = s // G, s % G
        scale = HD ** (-0.5)

        xg = jnp.concatenate([tokens, cotangent], axis=0)
        wa = pad_rows(jnp.concatenate([joint_weight.T, dense_weight], axis=0), 0)
        wb = pad_rows(jnp.concatenate([expand_weight.T, reduce_weight], axis=0), 0)
        vec = jnp.concatenate(
            [jnp.pad(array.astype(F32), (0, 128 - array.shape[0])) for array in (
                first_gain, first_shift, second_gain, second_shift, joint_bias, dense_bias,
                expand_bias, reduce_bias)]
        ).reshape(8, 128)
        xg_all, wa_all, wb_all, vec_all = gather_phase(N, F, G, xg, wa, wb, vec)

        va = vec_all.reshape(N * F, 1024)
        gain1, shift1, gain2, shift2, _, bias_d, _, bias_r = [
            va[:, 128 * i:128 * i + cd].reshape(D) for i in range(8)
        ]
        bias_j = lax.dynamic_slice_in_dim(va[:, 512:512 + cj], grp * G * F, G * F, 0).reshape(HG, 3, HD)
        bias_e = lax.dynamic_slice_in_dim(va[:, 768:768 + ce], s * F, F, 0).reshape(F * ce)

        joint = wa_all[:, :, :cj].reshape(HG, 3, HD, D)
        wq, wk, wv = [joint[:, i].reshape(W, D) for i in range(3)]
        dense = wa_all[:, :, cj:cj + cd].reshape(W, D)
        expand = wb_all[:, :ce].reshape(F * ce, D)
        reduce_w = wb_all[:, ce:2 * ce].reshape(F * ce, D)

        x = xg_all[:, 0].reshape(L, D).astype(F32)
        grad = xg_all[:, 1].reshape(L, D)
        center = x - jnp.mean(x, axis=-1, keepdims=True)
        inv = lax.rsqrt(jnp.mean(center * center, axis=-1, keepdims=True) + EPS)
        n = center * inv
        nf1 = (n * gain1 + shift1).astype(BF)
        nf2 = (n * gain2 + shift2).astype(BF)

        def mine(array):
            return lax.dynamic_slice_in_dim(array, gi * Q, Q, 0)

        def own_rows(array):
            pick = (jnp.arange(G) == gi)[:, None, None]
            return jnp.where(pick, array[None], 0.0).reshape(L, D)

        places = row_places(pair_held, L, R // 2)
        freq = 1.0 / 10000.0 ** (jnp.arange(0, ROT, 2, dtype=F32) / ROT)
        angles = places.astype(F32)[:, None] * freq[None, :]
        cosine, sine = jnp.cos(angles)[:, None], jnp.sin(angles)[:, None]
        cos_q, sin_q, places_q = mine(cosine), mine(sine), mine(places)

        nf1_q, grad_q = mine(nf1), mine(grad)
        q = turn(nt(nf1_q, wq).reshape(Q, HG, HD) + bias_j[:, 0], cos_q, sin_q).astype(BF)
        k = turn(nt(nf1, wk).reshape(L, HG, HD) + bias_j[:, 1], cosine, sine).astype(BF)
        v = (nt(nf1, wv).reshape(L, HG, HD) + bias_j[:, 2]).astype(BF)
        gctx = nt(grad_q, dense).astype(BF).reshape(Q, HG, HD)

        allowed = places_q[:, None] >= places[None, :]
        scores = jnp.einsum("qhd,khd->hqk", q, k, preferred_element_type=F32) * scale
        scores = jnp.where(allowed, scores, MASKED)
        peak = jnp.max(scores, axis=-1, keepdims=True)
        weight = jnp.exp(scores - peak)
        probs_full = weight / jnp.sum(weight, axis=-1, keepdims=True)
        probs = probs_full.astype(BF)
        context = jnp.einsum("hqk,khd->qhd", probs, v, preferred_element_type=F32)
        ctx_low = context.reshape(Q, W).astype(BF)
        g_probs = jnp.einsum("qhd,khd->hqk", gctx, v, preferred_element_type=F32)
        delta = jnp.sum(probs_full * g_probs, axis=-1, keepdims=True)
        g_scores = (probs_full * (g_probs - delta)).astype(BF)
        gq = jnp.einsum("hqk,khd->qhd", g_scores, k, preferred_element_type=F32) * scale
        gk = jnp.einsum("hqk,qhd->khd", g_scores, q, preferred_element_type=F32) * scale
        gv = jnp.einsum("hqk,qhd->khd", probs, gctx, preferred_element_type=F32)
        gq = turn(gq, cos_q, -sin_q).astype(BF).reshape(Q, W)
        gk = turn(gk, cosine, -sine).astype(BF).reshape(L, W)
        gv = gv.astype(BF).reshape(L, W)

        hidden = nt(nf2, expand) + bias_e
        active, gelu_pull = jax.vjp(lambda t: jax.nn.gelu(t, approximate=False), hidden)
        active = active.astype(BF)
        out_part = nn(active, reduce_w) + own_rows(nn(ctx_low, dense))
        g_hidden = gelu_pull(nt(grad, reduce_w))[0].astype(BF)
        g2 = nn(g_hidden, expand)
        g1 = nn(gk, wk) + nn(gv, wv) + own_rows(nn(gq, wq))
        t_part = g1 * gain1 + g2 * gain2

        d_joint = jnp.stack(
            [tn(gq, nf1_q).astype(BF).reshape(HG, HD, D), tn(gk, nf1).astype(BF).reshape(HG, HD, D),
             tn(gv, nf1).astype(BF).reshape(HG, HD, D)], axis=1
        ).reshape(G, F, cj, D)
        d_dense = tn(ctx_low, grad_q).astype(BF).reshape(G, F, cd, D)
        ga = pad_rows(jnp.concatenate([d_joint, d_dense], axis=2), 2)
        gb = pad_rows(
            jnp.concatenate(
                [tn(g_hidden, nf2).astype(BF).reshape(F, ce, D),
                 tn(active, grad).astype(BF).reshape(F, ce, D)], axis=1), 1
        )

        def col(array):
            return jnp.sum(array.astype(F32), axis=0)

        owner_s = jnp.arange(N * F) // F
        gains = [
            p.reshape(N * F, cd)
            for p in (jnp.sum(g1 * n, axis=0), jnp.sum(g1, axis=0), jnp.sum(g2 * n, axis=0), jnp.sum(g2, axis=0))
        ]
        b_joint = jnp.stack([col(a).reshape(HG, HD) for a in (gq, gk, gv)], axis=1).reshape(G * F, cj)
        b_joint = lax.dynamic_update_slice_in_dim(jnp.zeros((N * F, cj), F32), b_joint, grp * G * F, 0)
        b_expand = lax.dynamic_update_slice_in_dim(
            jnp.zeros((N * F, ce), F32), col(g_hidden).reshape(F, ce), s * F, 0
        )
        b_out = jnp.where((owner_s == s)[:, None], col(grad).reshape(N * F, cd), 0.0)
        vecp = jnp.concatenate(gains + [b_joint, b_out, b_expand], axis=1)
        vecp = jnp.pad(vecp, ((0, 0), (0, 1024 - vecp.shape[1]))).reshape(N, F, 8, 128)

        outr, tr, gar, gbr, vecr = scatter_phase(
            N, F, G, out_part.astype(BF).reshape(N, R, D), t_part.astype(BF).reshape(N, R, D),
            ga, gb, vecp
        )
        x_own = tokens[0].astype(F32)
        layer_output = (x_own + jnp.sum(outr.astype(F32), axis=0) + bias_d + bias_r).astype(BF)
        center = x_own - jnp.mean(x_own, axis=-1, keepdims=True)
        inv_own = lax.rsqrt(jnp.mean(center * center, axis=-1, keepdims=True) + EPS)
        n_own = center * inv_own
        t = jnp.sum(tr.astype(F32), axis=0)
        g_in = (
            t - jnp.mean(t, axis=-1, keepdims=True)
            - n_own * jnp.mean(t * n_own, axis=-1, keepdims=True)
        ) * inv_own
        input_grad = (cotangent[0].astype(F32) + g_in).astype(BF)
        a = jnp.sum(gar.astype(F32), axis=0)
        b = jnp.sum(gbr.astype(F32), axis=0)
        vs = jnp.sum(vecr, axis=0).reshape(1024)
        at = 4 * cd
        o_joint, at = vs[at:at + cj], at + cj
        o_out, at = vs[at:at + cd], at + cd
        o_expand = vs[at:at + ce]
        return (
            layer_output[None], input_grad[None], a[:cj].T, o_joint, a[cj:cj + cd], o_out,
            b[:ce].T, o_expand, b[ce:2 * ce], o_out,
            vs[:cd], vs[cd:2 * cd], vs[2 * cd:3 * cd], vs[3 * cd:4 * cd],
        )

    return body


def solution(mesh):
    both = ("seq", "fsdp")
    cols, rows, vector = P(None, both), P(both, None), P(both)
    acts = P("fsdp", "seq", None)
    return jax.shard_map(
        make_body(mesh.shape["seq"], mesh.shape["fsdp"]),
        mesh=mesh,
        in_specs=(
            acts, P(), cols, vector, rows, vector, cols, vector, rows, vector,
            vector, vector, vector, vector, acts,
        ),
        out_specs=(
            acts, acts, cols, vector, rows, vector, cols, vector, rows, vector,
            vector, vector, vector, vector,
        ),
        check_vma=False,
    )
```
